32 devices in a mesh: rep: 2 (over y), row: 4 (over z), col: 4 (over x, core).
Axes of the slice: x: 2, y: 2, z: 4, core: 2. Of those that a mesh axis runs over, the one named last changes fastest.
Arguments:
- tokens: bfloat16 [192, 8192], P(('rep', 'row'), 'col'), parts along dimension 0, may hold values from -6 to 6
- w_up: bfloat16 [8192, 16384], P('col', 'row'), may hold values from -0.0625 to 0.0625
- w_down: bfloat16 [16384, 8192], P('row', 'col'), may hold values from -0.046875 to 0.046875
- upstream: bfloat16 [192, 8192], P(('rep', 'row'), 'col'), parts along dimension 0, may hold values from -6 to 6
Outputs:
- layer_out: bfloat16 [192, 8192], P(('rep', 'row'), 'col'), parts along dimension 0
- grad_tokens: bfloat16 [192, 8192], P(('rep', 'row'), 'col'), parts along dimension 0
- grad_up: bfloat16 [16384, 16384], P(('rep', 'col'), 'row'), parts along dimension 0
- grad_down: bfloat16 [32768, 8192], P(('rep', 'row'), 'col'), parts along dimension 0
The draws below stay inside these ranges and needn't reach their ends.
There are 2 independent parts, one for each index of `rep`. The reference program is written for one: setup_inputs(seed, part) draws one part's arguments, and reference() takes and returns one part's arrays. A program takes and returns all parts, laid end to end along the dimension named above; an argument that names none is the same for every part. Nothing has to cross between parts.
All inputs are finite; a program needn't handle non-finite values.
Results may differ from the reference program's by a relative error of at most 0.0051.
Values may be sent and summed in bfloat16 or wider, within the bound.
A program may use at most 192 MiB of HBM per device.

```python
import jax
import jax.numpy as jnp
from jax import lax

D = 8192
FF = 16384
TOKENS = 96


def block_scale(own_key, shape, cuts, low, top_value):
    gain = 1.0
    for dim, parts in cuts:
        heights = jax.random.uniform(jax.random.fold_in(jax.random.fold_in(own_key, 6), dim), (parts,), jnp.float32, low / len(cuts), top_value / len(cuts))
        gain = gain * jnp.repeat(jnp.exp(heights), shape[dim] // parts).reshape((-1,) + (1,) * (len(shape) - 1 - dim))
    return gain


def noise(rng, shape, spread, most, split=(), kind=jnp.bfloat16):
    factor_of = block_scale(rng, shape, split, -0.22, 0.18) if split else 1.0
    drawn = jax.random.normal(rng, shape, jnp.float32) * spread * factor_of
    return jnp.minimum(jnp.maximum(drawn, -most), most).astype(kind)


def setup_inputs(seed: int = 0, part: int = 0) -> dict:
    streams_of = jax.random.split(jax.random.key(seed), 5)
    part_splits = jax.random.split(jax.random.fold_in(streams_of[4], part), 5)
    return {
        "tokens": noise(part_splits[0], (TOKENS, D), 1.0, 6.0, ((0, 4), (1, 4))),
        "w_up": noise(streams_of[1], (D, FF), D ** -0.5, 0.0625, ((0, 4), (1, 4))),
        "w_down": noise(streams_of[2], (FF, D), FF ** -0.5, 0.046875, ((0, 4), (1, 4))),
        "upstream": noise(part_splits[3], (TOKENS, D), 1.0, 6.0, ((0, 4), (1, 4))),
    }


root_half = 0.7071067811865476
inv_root_tau = 0.3989422804014327


def gelu_value(values):
    return 0.5 * values * (1.0 + lax.erf(values * root_half))


def gelu_slope(values):
    return 0.5 * (1.0 + lax.erf(values * root_half)) + values * jnp.exp(-0.5 * values * values) * inv_root_tau


def reference(tokens, w_up, w_down, upstream):
    hidden = jnp.dot(tokens, w_up, preferred_element_type=jnp.float32)
    activated = gelu_value(hidden).astype(jnp.bfloat16)
    layer_out = jnp.dot(activated, w_down, preferred_element_type=jnp.float32).astype(jnp.bfloat16)
    d_act = jnp.dot(upstream, w_down.T, preferred_element_type=jnp.float32)
    d_hidden = (d_act * gelu_slope(hidden)).astype(jnp.bfloat16)
    factor = TOKENS ** -0.5
    grad_down = (jnp.dot(activated.T, upstream, preferred_element_type=jnp.float32) * factor).astype(jnp.bfloat16)
    grad_up = (jnp.dot(tokens.T, d_hidden, preferred_element_type=jnp.float32) * factor).astype(jnp.bfloat16)
    grad_tokens = jnp.dot(d_hidden, w_up.T, preferred_element_type=jnp.float32).astype(jnp.bfloat16)
    return (layer_out, grad_tokens, grad_up, grad_down)
```

```python
import functools

import jax
import jax.numpy as jnp
from jax import lax
from jax.experimental import pallas as pl
from jax.experimental.pallas import tpu as pltpu
from jax.sharding import PartitionSpec as P

MESH = pl.DeviceIdType.MESH
F32, BF16 = jnp.float32, jnp.bfloat16
root_half = 0.7071067811865476
inv_root_tau = 0.3989422804014327


def gelu_value(values):
    return 0.5 * values * (1.0 + lax.erf(values * root_half))


def gelu_slope(values):
    return (
        0.5 * (1.0 + lax.erf(values * root_half))
        + values * jnp.exp(-0.5 * values * values) * inv_root_tau
    )


def contract_rows(left, right):
    return lax.dot_general(left, right, (((0,), (0,)), ((), ())), preferred_element_type=F32)


def contract_cols(left, right):
    return lax.dot_general(left, right, (((1,), (1,)), ((), ())), preferred_element_type=F32)


def remote(src, dst, send, recv, where):
    return pltpu.make_async_remote_copy(
        src_ref=src, dst_ref=dst, send_sem=send, recv_sem=recv,
        device_id=where, device_id_type=MESH,
    )


def exchange_kernel(
    n, chunks, half, tile,
    tok_in, up_in, down_in, cot_in,
    lay_out, gtok_out, tok_out, cot_out, act_out, dh_out,
    wu, wd, tblk, cblk, tok, cot,
    hp, dp, hc, dc, hs, ds_, hx, dx, act, dh,
    lo, gt, lob, gtb, lor, gtr, lfin, gfin,
    wu_sem, wd_sem, own_sem, out_sem,
    t_send, t_recv, c_send, c_recv,
    core_send, core_recv, x_send, x_recv, a_send, a_recv, r_send, r_recv,
):
    row = lax.axis_index("row")
    col = lax.axis_index("col")
    bit = lax.rem(col, 2)
    mate = {"col": col + 1 - 2 * bit}
    across = {"col": lax.rem(col + 2, 4)}
    rows = tok_in.shape[0]
    width = tok_in.shape[1]
    tiles = width // tile

    up_copies = [
        pltpu.make_async_copy(up_in.at[:, pl.ds(g * half, half)], wu.at[g], wu_sem.at[g])
        for g in range(2 * chunks)
    ]
    down_copies = [
        pltpu.make_async_copy(down_in.at[pl.ds(g * half, half), :], wd.at[g], wd_sem.at[g])
        for g in range(2 * chunks)
    ]
    own_t = pltpu.make_async_copy(tok_in, tblk.at[row], own_sem.at[0])
    own_c = pltpu.make_async_copy(cot_in, cblk.at[row], own_sem.at[1])
    own_t.start()
    own_c.start()
    for copy in up_copies:
        copy.start()

    barrier = pltpu.get_barrier_semaphore()
    for step in range(1, n):
        pl.semaphore_signal(
            barrier, inc=1, device_id={"row": lax.rem(row + step, n)}, device_id_type=MESH
        )
    pl.semaphore_signal(barrier, inc=1, device_id=mate, device_id_type=MESH)
    pl.semaphore_signal(barrier, inc=1, device_id=across, device_id_type=MESH)
    pl.semaphore_wait(barrier, n + 1)

    right = {"row": lax.rem(row + 1, n)}
    left = {"row": lax.rem(row + n - 1, n)}

    def send_own(src, blk, send, recv):
        @pl.when(row < n - 1)
        def _():
            remote(src, blk.at[row], send.at[0, row], recv.at[row], right).start()

        @pl.when(row > 0)
        def _():
            remote(src, blk.at[row], send.at[1, row], recv.at[row], left).start()

    def hop(step, blk, send, recv):
        low, high = row - step, row + step

        @pl.when(low >= 0)
        def _():
            remote(blk.at[low], blk.at[low], send.at[0, low], recv.at[low], right).wait_recv()

            @pl.when(row < n - 1)
            def _():
                remote(blk.at[low], blk.at[low], send.at[0, low], recv.at[low], right).start()

        @pl.when(high < n)
        def _():
            remote(blk.at[high], blk.at[high], send.at[1, high], recv.at[high], left).wait_recv()

            @pl.when(row > 0)
            def _():
                remote(blk.at[high], blk.at[high], send.at[1, high], recv.at[high], left).start()

    def close_hops(src, blk, send, recv):
        for b in range(n):
            @pl.when(jnp.logical_and(b <= row, row < n - 1))
            def _():
                remote(blk.at[b], blk.at[b], send.at[0, b], recv.at[b], right).wait_send()

            @pl.when(jnp.logical_and(b >= row, row > 0))
            def _():
                remote(blk.at[b], blk.at[b], send.at[1, b], recv.at[b], left).wait_send()

    def join(blk, whole):
        whole[...] = jnp.concatenate(
            [blk[b].astype(F32) for b in range(n)], axis=0
        ).astype(BF16)

    send_own(tok_in, tblk, t_send, t_recv)
    for step in range(1, n):
        hop(step, tblk, t_send, t_recv)
        if step == n - 2:
            send_own(cot_in, cblk, c_send, c_recv)
    if n < 3:
        send_own(cot_in, cblk, c_send, c_recv)
    for copy in down_copies:
        copy.start()
    own_t.wait()
    join(tblk, tok)
    tok_save = pltpu.make_async_copy(tok, tok_out, out_sem.at[0])
    tok_save.start()

    def to_mate(which, k, part, landing):
        return remote(
            part.at[k, 1 - bit], landing.at[k], core_send.at[which, k], core_recv.at[which, k], mate
        )

    def to_across(which, k, sent, landing):
        return remote(
            sent.at[k], landing.at[k], x_send.at[which, k], x_recv.at[which, k], across
        )

    def to_share(which, k, value):
        return remote(
            value.at[k, bit], value.at[k, bit], a_send.at[which, k], a_recv.at[which, k], mate
        )

    def from_share(which, k, value):
        return remote(
            value.at[k, 1 - bit], value.at[k, 1 - bit],
            a_send.at[which, k], a_recv.at[which, k], mate,
        )

    def pair_sum(which, k, part, landing, sent, arrive):
        to_mate(which, k, part, landing).wait_recv()
        total = part[k, bit] + landing[k]
        part[k, bit] = total
        sent[k] = total.astype(BF16)
        to_across(which, k, sent, arrive).start()

    def finish_hidden(k):
        to_across(0, k, hs, hx).wait_recv()
        hidden = hp[k, bit] + hx[k].astype(F32)
        hp[k, bit] = hidden
        act[k, bit] = gelu_value(hidden).astype(BF16)
        to_share(0, k, act).start()

    def finish_slope(k):
        to_across(1, k, ds_, dx).wait_recv()
        d_act = dp[k, bit] + dx[k].astype(F32)
        dh[k, bit] = (d_act * gelu_slope(hp[k, bit])).astype(BF16)
        to_share(1, k, dh).start()

    for k in range(chunks):
        up_copies[2 * k].wait()
        up_copies[2 * k + 1].wait()
        hp[k, 1 - bit] = jnp.dot(tok[...], wu[2 * k + 1 - bit], preferred_element_type=F32)
        to_mate(0, k, hp, hc).start()
        hp[k, bit] = jnp.dot(tok[...], wu[2 * k + bit], preferred_element_type=F32)
        if 1 <= k + 1 < n and k + 1 <= n - 1:
            hop(k + 1, cblk, c_send, c_recv)
        if k >= 1:
            pair_sum(0, k - 1, hp, hc, hs, hx)
    for step in range(chunks + 1, n):
        hop(step, cblk, c_send, c_recv)
    pair_sum(0, chunks - 1, hp, hc, hs, hx)
    own_c.wait()
    join(cblk, cot)
    cot_save = pltpu.make_async_copy(cot, cot_out, out_sem.at[1])
    cot_save.start()

    for k in range(chunks):
        down_copies[2 * k].wait()
        down_copies[2 * k + 1].wait()
        dp[k, 1 - bit] = contract_cols(cot[...], wd[2 * k + 1 - bit])
        to_mate(1, k, dp, dc).start()
        dp[k, bit] = contract_cols(cot[...], wd[2 * k + bit])
        if k >= 1:
            pair_sum(1, k - 1, dp, dc, ds_, dx)
            finish_hidden(k - 1)
    pair_sum(1, chunks - 1, dp, dc, ds_, dx)
    finish_hidden(chunks - 1)

    def scatter(which, total, out_blk, landing):
        for j in range(tiles):
            for b in range(n):
                out_blk[b, :, pl.ds(j * tile, tile)] = total[j, b * rows:(b + 1) * rows, :].astype(BF16)
        for step in range(1, n):
            to = lax.rem(row + step, n)
            remote(
                out_blk.at[to], landing.at[row],
                r_send.at[which, step], r_recv.at[which, row], {"row": to},
            ).start()

    def collect(which, total, out_blk, landing, final, out, sem):
        for step in range(1, n):
            frm = lax.rem(row + n - step, n)
            remote(
                out_blk.at[frm], landing.at[frm],
                r_send.at[which, step], r_recv.at[which, frm], {"row": frm},
            ).wait_recv()
        for j in range(tiles):
            cols = pl.ds(j * tile, tile)
            value = total[j, pl.ds(pl.multiple_of(row * rows, 8), rows), :]
            for step in range(1, n):
                value = value + landing[lax.rem(row + n - step, n), :, cols].astype(F32)
            final[:, cols] = value.astype(BF16)
        save = pltpu.make_async_copy(final, out, sem)
        save.start()
        return save

    for k in range(chunks):
        from_share(0, k, act).wait_recv()

        @pl.loop(0, tiles)
        def _(j, k=k):
            cols = pl.ds(pl.multiple_of(j * tile, tile), tile)
            term = jnp.dot(act[k, 0], wd[2 * k, :, cols], preferred_element_type=F32)
            term = term + jnp.dot(act[k, 1], wd[2 * k + 1, :, cols], preferred_element_type=F32)
            lo[j] = term if k == 0 else lo[j] + term
    act_save = pltpu.make_async_copy(act, act_out, out_sem.at[2])
    act_save.start()
    scatter(0, lo, lob, lor)

    finish_slope(0)
    for k in range(chunks):
        if k + 1 < chunks:
            finish_slope(k + 1)
        from_share(1, k, dh).wait_recv()

        @pl.loop(0, tiles)
        def _(j, k=k):
            at = pl.ds(pl.multiple_of(j * tile, tile), tile)
            term = contract_cols(dh[k, 0], wu[2 * k, at, :])
            term = term + contract_cols(dh[k, 1], wu[2 * k + 1, at, :])
            gt[j] = term if k == 0 else gt[j] + term
    dh_save = pltpu.make_async_copy(dh, dh_out, out_sem.at[3])
    dh_save.start()
    scatter(1, gt, gtb, gtr)
    lay_save = collect(0, lo, lob, lor, lfin, lay_out, out_sem.at[4])
    gtok_save = collect(1, gt, gtb, gtr, gfin, gtok_out, out_sem.at[5])

    close_hops(tok_in, tblk, t_send, t_recv)
    close_hops(cot_in, cblk, c_send, c_recv)
    for k in range(chunks):
        to_mate(0, k, hp, hc).wait_send()
        to_mate(1, k, dp, dc).wait_send()
        to_across(0, k, hs, hx).wait_send()
        to_across(1, k, ds_, dx).wait_send()
        to_share(0, k, act).wait_send()
        to_share(1, k, dh).wait_send()
    for which, blk in ((0, lob), (1, gtb)):
        for step in range(1, n):
            to = lax.rem(row + step, n)
            remote(
                blk.at[to], blk.at[to],
                r_send.at[which, step], r_recv.at[which, row], {"row": to},
            ).wait_send()
    for save in (tok_save, cot_save, act_save, dh_save, lay_save, gtok_save):
        save.wait()


def grads_kernel(factor, tok, cot, act, dh, up, down, tok_turned):
    @pl.when(pl.program_id(0) == 0)
    def _():
        tok_turned[...] = tok[...].T

    down[...] = (contract_rows(act[0], cot[...]) * factor).astype(BF16)
    up[...] = (jnp.dot(tok_turned[...], dh[0], preferred_element_type=F32) * factor).astype(BF16)


def fused(tokens, w_up, w_down, upstream):
    n = lax.axis_size("row")
    rows, width = tokens.shape
    units = w_up.shape[1]
    count = rows * n
    half = 512
    chunks = units // (2 * half)
    tile = 512
    tiles = width // tile
    dma = pltpu.SemaphoreType.DMA
    anywhere = pl.BlockSpec(memory_space=pl.ANY)
    part = (chunks, 2, count, half)
    own = (chunks, count, half)
    scratch = [
        pltpu.VMEM((2 * chunks, width, half), BF16),
        pltpu.VMEM((2 * chunks, half, width), BF16),
        pltpu.VMEM((n, rows, width), BF16),
        pltpu.VMEM((n, rows, width), BF16),
        pltpu.VMEM((count, width), BF16),
        pltpu.VMEM((count, width), BF16),
        pltpu.VMEM(part, F32),
        pltpu.VMEM(part, F32),
        pltpu.VMEM(own, F32),
        pltpu.VMEM(own, F32),
        pltpu.VMEM(own, BF16),
        pltpu.VMEM(own, BF16),
        pltpu.VMEM(own, BF16),
        pltpu.VMEM(own, BF16),
        pltpu.VMEM(part, BF16),
        pltpu.VMEM(part, BF16),
        pltpu.VMEM((tiles, count, tile), F32),
        pltpu.VMEM((tiles, count, tile), F32),
        pltpu.VMEM((n, rows, width), BF16),
        pltpu.VMEM((n, rows, width), BF16),
        pltpu.VMEM((n, rows, width), BF16),
        pltpu.VMEM((n, rows, width), BF16),
        pltpu.VMEM((rows, width), BF16),
        pltpu.VMEM((rows, width), BF16),
        dma((2 * chunks,)),
        dma((2 * chunks,)),
        dma((2,)),
        dma((6,)),
        dma((2, n)),
        dma((n,)),
        dma((2, n)),
        dma((n,)),
        dma((2, chunks)),
        dma((2, chunks)),
        dma((2, chunks)),
        dma((2, chunks)),
        dma((2, chunks)),
        dma((2, chunks)),
        dma((2, n)),
        dma((2, n)),
    ]
    shape = jax.ShapeDtypeStruct
    layer, grad_tokens, tok, cot, act, dh = pl.pallas_call(
        functools.partial(exchange_kernel, n, chunks, half, tile),
        out_shape=[
            shape((rows, width), BF16),
            shape((rows, width), BF16),
            shape((count, width), BF16),
            shape((count, width), BF16),
            shape(part, BF16),
            shape(part, BF16),
        ],
        in_specs=[anywhere] * 4,
        out_specs=[anywhere] * 6,
        scratch_shapes=scratch,
        compiler_params=pltpu.CompilerParams(
            collective_id=0, has_side_effects=True, vmem_limit_bytes=60 * 1024 * 1024
        ),
        cost_estimate=pl.CostEstimate(
            flops=8 * count * width * units,
            bytes_accessed=4 * width * units,
            transcendentals=0,
        ),
    )(tokens, w_up, w_down, upstream)
    act = act.reshape(2 * chunks, count, half)
    dh = dh.reshape(2 * chunks, count, half)
    step = 256
    per = half // step
    whole = pl.BlockSpec((count, width), lambda g: (0, 0))
    grad_up, grad_down = pl.pallas_call(
        functools.partial(grads_kernel, count ** (-0.5)),
        grid=(units // step,),
        out_shape=[shape((width, units), BF16), shape((units, width), BF16)],
        in_specs=[
            whole,
            whole,
            pl.BlockSpec((1, count, step), lambda g: (g // per, 0, g % per)),
            pl.BlockSpec((1, count, step), lambda g: (g // per, 0, g % per)),
        ],
        out_specs=[
            pl.BlockSpec((width, step), lambda g: (0, g)),
            pl.BlockSpec((step, width), lambda g: (g, 0)),
        ],
        scratch_shapes=[pltpu.VMEM((width, count), BF16)],
        compiler_params=pltpu.CompilerParams(vmem_limit_bytes=32 * 1024 * 1024),
        cost_estimate=pl.CostEstimate(
            flops=4 * count * width * units,
            bytes_accessed=4 * width * units,
            transcendentals=0,
        ),
    )(tok, cot, act, dh)
    return layer, grad_tokens, grad_up, grad_down


def plain(tokens, w_up, w_down, upstream):
    gathered = lax.all_gather(tokens, "row", axis=0, tiled=True)
    gathered_grad = lax.all_gather(upstream, "row", axis=0, tiled=True)
    factor = gathered.shape[0] ** (-0.5)
    hidden = lax.psum(jnp.dot(gathered, w_up, preferred_element_type=F32), "col")
    activated = gelu_value(hidden).astype(BF16)
    layer_part = lax.psum_scatter(
        jnp.dot(activated, w_down, preferred_element_type=F32),
        "row", scatter_dimension=0, tiled=True,
    )
    d_act = lax.psum(contract_cols(gathered_grad, w_down), "col")
    d_hidden = (d_act * gelu_slope(hidden)).astype(BF16)
    grad_down = (contract_rows(activated, gathered_grad) * factor).astype(BF16)
    grad_up = (contract_rows(gathered, d_hidden) * factor).astype(BF16)
    grad_part = lax.psum_scatter(
        contract_cols(d_hidden, w_up), "row", scatter_dimension=0, tiled=True
    )
    return (layer_part.astype(BF16), grad_part.astype(BF16), grad_up, grad_down)


def shards(mesh, tokens, w_up, w_down, upstream):
    width, units = w_up.shape
    count = tokens.shape[0] * mesh.shape["row"]
    fits = (
        mesh.shape["col"] == 4
        and 2 <= mesh.shape["row"] <= 8
        and units % 1024 == 0
        and width % 512 == 0
        and count % 16 == 0
        and tokens.shape[0] % 8 == 0
        and 4 * width * units + 32 * count * units + 24 * count * width <= 56 * 2 ** 20
    )
    return (fused if fits else plain)(tokens, w_up, w_down, upstream)


def solution(mesh):
    placed = (P(("rep", "row"), "col"), P("col", "row"), P("row", "col"), P(("rep", "row"), "col"))
    return jax.shard_map(
        functools.partial(shards, mesh),
        mesh=mesh,
        in_specs=placed,
        out_specs=(
            P(("rep", "row"), "col"),
            P(("rep", "row"), "col"),
            P(("rep", "col"), "row"),
            P(("rep", "row"), "col"),
        ),
        check_vma=False,
    )
```

```python
import functools

import jax
import jax.numpy as jnp
from jax import lax
from jax.experimental import pallas as pl
from jax.experimental.pallas import tpu as pltpu
from jax.sharding import PartitionSpec as P

MESH = pl.DeviceIdType.MESH
F32, BF16 = jnp.float32, jnp.bfloat16
root_half = 0.7071067811865476
inv_root_tau = 0.3989422804014327


def gelu_value(values):
    return 0.5 * values * (1.0 + lax.erf(values * root_half))


def gelu_slope(values):
    return (
        0.5 * (1.0 + lax.erf(values * root_half))
        + values * jnp.exp(-0.5 * values * values) * inv_root_tau
    )


def contract_rows(left, right):
    return lax.dot_general(left, right, (((0,), (0,)), ((), ())), preferred_element_type=F32)


def contract_cols(left, right):
    return lax.dot_general(left, right, (((1,), (1,)), ((), ())), preferred_element_type=F32)


def remote(src, dst, send, recv, where):
    return pltpu.make_async_remote_copy(
        src_ref=src, dst_ref=dst, send_sem=send, recv_sem=recv,
        device_id=where, device_id_type=MESH,
    )


def exchange_kernel(
    n, chunks, half, tile,
    tok_in, up_in, down_in, cot_in,
    lay_out, tok_out, cot_out, act_out, dh_out, gtb_out, *scratch
):
    (
    wu, wd, tblk, cblk, tok, cot,
    hp, dp, hc, dc, hs, ds_, hx, dx, act, dh,
    lo, gt, lob, gtb, lor, lfin,
    wu_sem, wd_sem, own_sem, out_sem,
    t_send, t_recv, c_send, c_recv,
    core_send, core_recv, x_send, x_recv, a_send, a_recv, r_send, r_recv,
    ) = scratch
    row = lax.axis_index("row")
    col = lax.axis_index("col")
    bit = lax.rem(col, 2)
    mate = {"col": col + 1 - 2 * bit}
    across = {"col": lax.rem(col + 2, 4)}
    rows = tok_in.shape[0]
    width = tok_in.shape[1]
    tiles = width // tile

    up_copies = [
        pltpu.make_async_copy(up_in.at[:, pl.ds(g * half, half)], wu.at[g], wu_sem.at[g])
        for g in range(2 * chunks)
    ]
    down_copies = [
        pltpu.make_async_copy(down_in.at[pl.ds(g * half, half), :], wd.at[g], wd_sem.at[g])
        for g in range(2 * chunks)
    ]
    own_t = pltpu.make_async_copy(tok_in, tblk.at[row], own_sem.at[0])
    own_c = pltpu.make_async_copy(cot_in, cblk.at[row], own_sem.at[1])
    own_t.start()
    own_c.start()
    for copy in up_copies:
        copy.start()

    barrier = pltpu.get_barrier_semaphore()
    for step in range(1, n):
        pl.semaphore_signal(
            barrier, inc=1, device_id={"row": lax.rem(row + step, n)}, device_id_type=MESH
        )
    pl.semaphore_signal(barrier, inc=1, device_id=mate, device_id_type=MESH)
    pl.semaphore_signal(barrier, inc=1, device_id=across, device_id_type=MESH)
    pl.semaphore_wait(barrier, n + 1)

    def other(step):
        return lax.rem(row + step, n)

    def greet(step, src, blk, send, recv):
        to = other(step)
        return remote(src, blk.at[row], send.at[step], recv.at[row], {"row": to})

    def arrive(step, blk, send, recv):
        frm = other(step)
        remote(blk.at[frm], blk.at[frm], send.at[step], recv.at[frm], {"row": frm}).wait_recv()

    def join(blk, whole):
        whole[...] = jnp.concatenate(
            [blk[b].astype(F32) for b in range(n)], axis=0
        ).astype(BF16)

    for step in range(1, n):
        greet(step, tok_in, tblk, t_send, t_recv).start()
    for step in range(1, n):
        greet(step, cot_in, cblk, c_send, c_recv).start()
    for step in range(1, n):
        arrive(step, tblk, t_send, t_recv)
    for copy in down_copies:
        copy.start()
    own_t.wait()
    join(tblk, tok)
    tok_save = pltpu.make_async_copy(tok, tok_out, out_sem.at[0])
    tok_save.start()

    def to_mate(which, k, part, landing):
        return remote(
            part.at[k, 1 - bit], landing.at[k], core_send.at[which, k], core_recv.at[which, k], mate
        )

    def to_across(which, k, sent, landing):
        return remote(
            sent.at[k], landing.at[k], x_send.at[which, k], x_recv.at[which, k], across
        )

    def to_share(which, k, value):
        return remote(
            value.at[k, bit], value.at[k, bit], a_send.at[which, k], a_recv.at[which, k], mate
        )

    def from_share(which, k, value):
        return remote(
            value.at[k, 1 - bit], value.at[k, 1 - bit],
            a_send.at[which, k], a_recv.at[which, k], mate,
        )

    def pair_sum(which, k, part, landing, sent, arrive):
        to_mate(which, k, part, landing).wait_recv()
        total = part[k, bit] + landing[k]
        part[k, bit] = total
        sent[k] = total.astype(BF16)
        to_across(which, k, sent, arrive).start()

    def finish_hidden(k):
        to_across(0, k, hs, hx).wait_recv()
        hidden = hp[k, bit] + hx[k].astype(F32)
        hp[k, bit] = hidden
        act[k, bit] = gelu_value(hidden).astype(BF16)
        to_share(0, k, act).start()

    def finish_slope(k):
        to_across(1, k, ds_, dx).wait_recv()
        d_act = dp[k, bit] + dx[k].astype(F32)
        dh[k, bit] = (d_act * gelu_slope(hp[k, bit])).astype(BF16)
        to_share(1, k, dh).start()

    for k in range(chunks):
        up_copies[2 * k].wait()
        up_copies[2 * k + 1].wait()
        hp[k, 1 - bit] = jnp.dot(tok[...], wu[2 * k + 1 - bit], preferred_element_type=F32)
        to_mate(0, k, hp, hc).start()
        hp[k, bit] = jnp.dot(tok[...], wu[2 * k + bit], preferred_element_type=F32)
        if k >= 1:
            pair_sum(0, k - 1, hp, hc, hs, hx)
    pair_sum(0, chunks - 1, hp, hc, hs, hx)
    for step in range(1, n):
        arrive(step, cblk, c_send, c_recv)
    own_c.wait()
    join(cblk, cot)
    cot_save = pltpu.make_async_copy(cot, cot_out, out_sem.at[1])
    cot_save.start()

    for k in range(chunks):
        down_copies[2 * k].wait()
        down_copies[2 * k + 1].wait()
        dp[k, 1 - bit] = contract_cols(cot[...], wd[2 * k + 1 - bit])
        to_mate(1, k, dp, dc).start()
        dp[k, bit] = contract_cols(cot[...], wd[2 * k + bit])
        if k >= 1:
            pair_sum(1, k - 1, dp, dc, ds_, dx)
            finish_hidden(k - 1)
    pair_sum(1, chunks - 1, dp, dc, ds_, dx)
    finish_hidden(chunks - 1)

    def scatter(which, total, out_blk, landing):
        for j in range(tiles):
            for b in range(n):
                out_blk[b, :, pl.ds(j * tile, tile)] = total[j, b * rows:(b + 1) * rows, :].astype(BF16)
        for step in range(1, n):
            to = lax.rem(row + step, n)
            remote(
                out_blk.at[to], landing.at[row],
                r_send.at[which, step], r_recv.at[which, row], {"row": to},
            ).start()

    def collect(which, total, out_blk, landing, final, out, sem):
        for step in range(1, n):
            frm = lax.rem(row + n - step, n)
            remote(
                out_blk.at[frm], landing.at[frm],
                r_send.at[which, step], r_recv.at[which, frm], {"row": frm},
            ).wait_recv()
        for j in range(tiles):
            cols = pl.ds(j * tile, tile)
            value = total[j, pl.ds(pl.multiple_of(row * rows, 8), rows), :]
            for step in range(1, n):
                value = value + landing[lax.rem(row + n - step, n), :, cols].astype(F32)
            final[:, cols] = value.astype(BF16)
        save = pltpu.make_async_copy(final, out, sem)
        save.start()
        return save

    for k in range(chunks):
        from_share(0, k, act).wait_recv()

        @pl.loop(0, tiles)
        def _(j, k=k):
            cols = pl.ds(pl.multiple_of(j * tile, tile), tile)
            term = jnp.dot(act[k, 0], wd[2 * k, :, cols], preferred_element_type=F32)
            term = term + jnp.dot(act[k, 1], wd[2 * k + 1, :, cols], preferred_element_type=F32)
            lo[j] = term if k == 0 else lo[j] + term
    act_save = pltpu.make_async_copy(act, act_out, out_sem.at[2])
    act_save.start()
    scatter(0, lo, lob, lor)

    finish_slope(0)
    for k in range(chunks):
        if k + 1 < chunks:
            finish_slope(k + 1)
        from_share(1, k, dh).wait_recv()

        @pl.loop(0, tiles)
        def _(j, k=k):
            at = pl.ds(pl.multiple_of(j * tile, tile), tile)
            term = contract_cols(dh[k, 0], wu[2 * k, at, :])
            term = term + contract_cols(dh[k, 1], wu[2 * k + 1, at, :])
            gt[j] = term if k == 0 else gt[j] + term
    dh_save = pltpu.make_async_copy(dh, dh_out, out_sem.at[3])
    dh_save.start()
    for j in range(tiles):
        for b in range(n):
            gtb[b, :, pl.ds(j * tile, tile)] = gt[j, b * rows:(b + 1) * rows, :].astype(BF16)
    gtb_save = pltpu.make_async_copy(gtb, gtb_out, out_sem.at[5])
    gtb_save.start()
    lay_save = collect(0, lo, lob, lor, lfin, lay_out, out_sem.at[4])

    for step in range(1, n):
        greet(step, tok_in, tblk, t_send, t_recv).wait_send()
        greet(step, cot_in, cblk, c_send, c_recv).wait_send()
    for k in range(chunks):
        to_mate(0, k, hp, hc).wait_send()
        to_mate(1, k, dp, dc).wait_send()
        to_across(0, k, hs, hx).wait_send()
        to_across(1, k, ds_, dx).wait_send()
        to_share(0, k, act).wait_send()
        to_share(1, k, dh).wait_send()
    for which, blk in ((0, lob),):
        for step in range(1, n):
            to = lax.rem(row + step, n)
            remote(
                blk.at[to], blk.at[to],
                r_send.at[which, step], r_recv.at[which, row], {"row": to},
            ).wait_send()
    for save in (tok_save, cot_save, act_save, dh_save, lay_save, gtb_save):
        save.wait()


def grads_kernel(factor, tok, cot, act, dh, lay, up, down, lay_out):
    @pl.when(pl.program_id(0) == 0)
    def _():
        lay_out[...] = lay[...]

    down[...] = (contract_rows(act[0], cot[...]) * factor).astype(BF16)
    turned = tok[...].T
    half = dh.shape[2]
    for g in range(dh.shape[0]):
        value = jnp.dot(turned, dh[g], preferred_element_type=F32)
        up[:, g * half:(g + 1) * half] = (value * factor).astype(BF16)


def fused(tokens, w_up, w_down, upstream):
    n = lax.axis_size("row")
    rows, width = tokens.shape
    units = w_up.shape[1]
    count = rows * n
    half = 512
    chunks = units // (2 * half)
    tile = 512
    tiles = width // tile
    dma = pltpu.SemaphoreType.DMA
    anywhere = pl.BlockSpec(memory_space=pl.ANY)
    part = (chunks, 2, count, half)
    own = (chunks, count, half)
    scratch = [
        pltpu.VMEM((2 * chunks, width, half), BF16),
        pltpu.VMEM((2 * chunks, half, width), BF16),
        pltpu.VMEM((n, rows, width), BF16),
        pltpu.VMEM((n, rows, width), BF16),
        pltpu.VMEM((count, width), BF16),
        pltpu.VMEM((count, width), BF16),
        pltpu.VMEM(part, F32),
        pltpu.VMEM(part, F32),
        pltpu.VMEM(own, F32),
        pltpu.VMEM(own, F32),
        pltpu.VMEM(own, BF16),
        pltpu.VMEM(own, BF16),
        pltpu.VMEM(own, BF16),
        pltpu.VMEM(own, BF16),
        pltpu.VMEM(part, BF16),
        pltpu.VMEM(part, BF16),
        pltpu.VMEM((tiles, count, tile), F32),
        pltpu.VMEM((tiles, count, tile), F32),
        pltpu.VMEM((n, rows, width), BF16),
        pltpu.VMEM((n, rows, width), BF16),
        pltpu.VMEM((n, rows, width), BF16),
        pltpu.VMEM((rows, width), BF16),
        dma((2 * chunks,)),
        dma((2 * chunks,)),
        dma((2,)),
        dma((6,)),
        dma((n,)),
        dma((n,)),
        dma((n,)),
        dma((n,)),
        dma((2, chunks)),
        dma((2, chunks)),
        dma((2, chunks)),
        dma((2, chunks)),
        dma((2, chunks)),
        dma((2, chunks)),
        dma((2, n)),
        dma((2, n)),
    ]
    shape = jax.ShapeDtypeStruct
    layer, tok, cot, act, dh, partial = pl.pallas_call(
        functools.partial(exchange_kernel, n, chunks, half, tile),
        out_shape=[
            shape((rows, width), BF16),
            shape((count, width), BF16),
            shape((count, width), BF16),
            shape(part, BF16),
            shape(part, BF16),
            shape((n, rows, width), BF16),
        ],
        in_specs=[anywhere] * 4,
        out_specs=[anywhere] * 6,
        scratch_shapes=scratch,
        compiler_params=pltpu.CompilerParams(
            collective_id=0, has_side_effects=True, vmem_limit_bytes=60 * 1024 * 1024
        ),
        cost_estimate=pl.CostEstimate(
            flops=8 * count * width * units,
            bytes_accessed=4 * width * units,
            transcendentals=0,
        ),
    )(tokens, w_up, w_down, upstream)
    landed = lax.all_to_all(partial, "row", 0, 0, tiled=True)
    act = act.reshape(2 * chunks, count, half)
    dh = dh.reshape(2 * chunks, count, half)
    steps = 2 * chunks
    wide = width // steps
    block = pl.BlockSpec((rows, width), lambda g: (0, 0))
    grad_up, grad_down, layer = pl.pallas_call(
        functools.partial(grads_kernel, count ** (-0.5)),
        grid=(steps,),
        out_shape=[
            shape((width, units), BF16),
            shape((units, width), BF16),
            shape((rows, width), BF16),
        ],
        in_specs=[
            pl.BlockSpec((count, wide), lambda g: (0, g)),
            pl.BlockSpec((count, width), lambda g: (0, 0)),
            pl.BlockSpec((1, count, half), lambda g: (g, 0, 0)),
            pl.BlockSpec((steps, count, half), lambda g: (0, 0, 0)),
            block,
        ],
        out_specs=[
            pl.BlockSpec((wide, units), lambda g: (g, 0)),
            pl.BlockSpec((half, width), lambda g: (g, 0)),
            block,
        ],
        compiler_params=pltpu.CompilerParams(vmem_limit_bytes=60 * 1024 * 1024),
        cost_estimate=pl.CostEstimate(
            flops=4 * count * width * units,
            bytes_accessed=4 * width * units,
            transcendentals=0,
        ),
    )(tok, cot, act, dh, layer)
    grad_tokens = jnp.sum(landed.astype(F32), axis=0).astype(BF16)
    return layer, grad_tokens, grad_up, grad_down


def plain(tokens, w_up, w_down, upstream):
    gathered = lax.all_gather(tokens, "row", axis=0, tiled=True)
    gathered_grad = lax.all_gather(upstream, "row", axis=0, tiled=True)
    factor = gathered.shape[0] ** (-0.5)
    hidden = lax.psum(jnp.dot(gathered, w_up, preferred_element_type=F32), "col")
    activated = gelu_value(hidden).astype(BF16)
    layer_part = lax.psum_scatter(
        jnp.dot(activated, w_down, preferred_element_type=F32),
        "row", scatter_dimension=0, tiled=True,
    )
    d_act = lax.psum(contract_cols(gathered_grad, w_down), "col")
    d_hidden = (d_act * gelu_slope(hidden)).astype(BF16)
    grad_down = (contract_rows(activated, gathered_grad) * factor).astype(BF16)
    grad_up = (contract_rows(gathered, d_hidden) * factor).astype(BF16)
    grad_part = lax.psum_scatter(
        contract_cols(d_hidden, w_up), "row", scatter_dimension=0, tiled=True
    )
    return (layer_part.astype(BF16), grad_part.astype(BF16), grad_up, grad_down)


def shards(mesh, tokens, w_up, w_down, upstream):
    width, units = w_up.shape
    count = tokens.shape[0] * mesh.shape["row"]
    fits = (
        mesh.shape["col"] == 4
        and 2 <= mesh.shape["row"] <= 8
        and units % 1024 == 0
        and width % (128 * (units // 512)) == 0
        and width % 512 == 0
        and count % 16 == 0
        and tokens.shape[0] % 8 == 0
        and 4 * width * units + 32 * count * units + 24 * count * width <= 56 * 2 ** 20
    )
    return (fused if fits else plain)(tokens, w_up, w_down, upstream)


def solution(mesh):
    placed = (P(("rep", "row"), "col"), P("col", "row"), P("row", "col"), P(("rep", "row"), "col"))
    return jax.shard_map(
        functools.partial(shards, mesh),
        mesh=mesh,
        in_specs=placed,
        out_specs=(
            P(("rep", "row"), "col"),
            P(("rep", "row"), "col"),
            P(("rep", "col"), "row"),
            P(("rep", "row"), "col"),
        ),
        check_vma=False,
    )
```
